256 devices in a mesh: gx: 4 (over z_hi), gy: 4 (over z_lo, core), gz: 16 (over y, x).
Axes of the slice: x: 4, y: 4, z: 8 (z_hi: 4, z_lo: 2; z = z_hi * 2 + z_lo), core: 2. Of those that a mesh axis runs over, the one named last changes fastest.
Arguments:
- near_modes: float32 [4, 4, 64, 24, 512], P('gx', 'gy', 'gz'), may hold values from -0.375 to 0.375
- diag_blocks: float32 [4, 4, 64, 512, 512], P('gx', 'gy', 'gz'), may hold values from -1 to 4
- face_blocks: float32 [4, 4, 64, 6, 128, 512], P('gx', 'gy', 'gz'), may hold values from -0.5 to 0.5
- face_rows: int32 [4, 4, 64, 6, 128], P('gx', 'gy', 'gz'), may hold values from 0 to 511, as said below
- coarse_modes: float32 [4, 4, 64, 24, 24], P('gx', 'gy', 'gz'), may hold values from -0.15625 to 0.15625
Outputs:
- coarse1: float32 [4, 4, 64, 24, 168], P('gx', 'gy', 'gz')
- coarse2: float32 [4, 4, 24, 120], P('gx', 'gy')
The draws below stay inside these ranges and needn't reach their ends.
Inputs may be any that keep to these rules, and one draw needn't show every extreme that they name: `face_rows`: for every aggregate and face the 128 row numbers are distinct.
All inputs are finite; a program needn't handle non-finite values.
Results may differ from the reference program's by a relative error of at most 0.000057.
Values sent between devices are 32-bit elements; how exact they have to be, the bound alone decides.
A program may use at most 320 MiB of HBM per device.

```python
import math
import jax
import jax.numpy as jnp
from jax import lax

DOFS = 512
FACE = 128
MODES = 24
NZA = 64
N_GX = 4
N_GY = 4


def draw_diag_blocks(key, part):
    first_key, second_key = jax.random.split(jax.random.fold_in(key, 11))
    block_shape = (N_GX, N_GY, NZA, DOFS, DOFS)
    offdiag = jax.random.truncated_normal(first_key, -4.0, 4.0, block_shape, jnp.float32)
    diagonal = jnp.exp(jax.random.uniform(second_key, block_shape[:-1], jnp.float32, 0.0, math.log(4.0)))
    offdiag = offdiag * (0.5 / math.sqrt(DOFS))
    on_diag = lax.broadcasted_iota(jnp.int32, (DOFS, DOFS), 0) == lax.broadcasted_iota(jnp.int32, (DOFS, DOFS), 1)
    return jnp.where(on_diag, diagonal[..., :, None], offdiag).astype(jnp.float32)


def draw_face_rows(key, part):
    face_count = N_GX * N_GY * NZA * 6
    face_keys = jax.random.split(jax.random.fold_in(key, 23), face_count)
    chosen = jax.vmap(lambda face_key: jax.random.permutation(face_key, DOFS)[:FACE])(face_keys)
    return chosen.reshape(N_GX, N_GY, NZA, 6, FACE).astype(jnp.int32)


def shard_levels(rng, shape, pieces, least, high):
    gain, own = 1.0, jax.random.fold_in(rng, 6)
    for axis_at, blocks in pieces:
        steps = jnp.exp(jax.random.uniform(jax.random.fold_in(own, axis_at), (blocks,), jnp.float32, least / len(pieces), high / len(pieces)))
        gain = gain * jnp.repeat(steps, shape[axis_at] // blocks).reshape([-1 if axis == axis_at else 1 for axis in range(len(shape))])
    return gain


def noise(key, shape, spread, reach, shards=(), kind=jnp.bfloat16):
    level = shard_levels(key, shape, shards, -0.22, 0.18) if shards else 1.0
    values = jax.random.normal(key, shape, jnp.float32) * spread * level
    return jnp.minimum(jnp.maximum(values, -reach), reach).astype(kind)


def setup_inputs(seed: int = 0) -> dict:
    key_of = jax.random.split(jax.random.key(seed), 6)
    return {
        "near_modes": noise(key_of[0], (N_GX, N_GY, NZA, MODES, DOFS), (DOFS // 2) ** -0.5, 0.375, ((0, 4), (1, 4), (2, 16)), jnp.float32),
        "diag_blocks": draw_diag_blocks(jax.random.fold_in(key_of[5], 71), 0),
        "face_blocks": noise(key_of[2], (N_GX, N_GY, NZA, 6, FACE, DOFS), (DOFS // 4) ** -0.5, 0.5, ((0, 4), (1, 4), (2, 16)), jnp.float32),
        "face_rows": draw_face_rows(jax.random.fold_in(key_of[5], 71), 0),
        "coarse_modes": noise(key_of[4], (N_GX, N_GY, NZA, MODES, MODES), (MODES * NZA) ** -0.5, 0.15625, ((0, 4), (1, 4), (2, 16)), jnp.float32),
    }


HIGHEST = lax.Precision.HIGHEST
OMEGA_FINE = 2.0 / 3.0
OMEGA_COARSE = 1.0
EPSILON = 1e-6


def pad_grid(array_in):
    return jnp.pad(array_in, [(1, 1)] * 3 + [(0, 0)] * (array_in.ndim - 3))


def neighbours(padded):
    return jnp.stack([padded[:-2, 1:-1, 1:-1], padded[2:, 1:-1, 1:-1], padded[1:-1, :-2, 1:-1],
                      padded[1:-1, 2:, 1:-1], padded[1:-1, 1:-1, :-2], padded[1:-1, 1:-1, 2:]], axis=3)


def add_rows(target, face_terms, face_rows):
    for face_index in range(6):
        target = target.at[:, face_rows[face_index]].add(face_terms[face_index])
    return target


def pick_rows(matrix_in, face_rows):
    return matrix_in[:, face_rows]


def smooth_fine(modes, near, diag_blocks, face_blocks, face_rows):
    product = jnp.einsum("nkc,nrc->nkr", modes, diag_blocks, precision=HIGHEST)
    face_terms = jnp.einsum("nfkc,nfhc->nfkh", near, face_blocks, precision=HIGHEST)
    product = jax.vmap(add_rows)(product, face_terms, face_rows)
    diagonal = jnp.diagonal(diag_blocks, axis1=1, axis2=2)
    return modes - OMEGA_FINE * product / diagonal[:, None, :]


def galerkin_fine(smoothed, near_smoothed, diag_blocks, face_blocks, face_rows):
    applied = jnp.einsum("nkc,nrc->nkr", smoothed, diag_blocks, precision=HIGHEST)
    own_block = jnp.einsum("nir,njr->nij", smoothed, applied, precision=HIGHEST)
    picked = jax.vmap(pick_rows)(smoothed, face_rows)
    across = jnp.einsum("nfkc,nfhc->nfkh", near_smoothed, face_blocks, precision=HIGHEST)
    lateral = jnp.einsum("nifh,nfjh->nfij", picked, across, precision=HIGHEST)
    blocks = jnp.concatenate([own_block[:, None], lateral], axis=1)
    agg_count, modes_count = own_block.shape[0], own_block.shape[1]
    return jnp.transpose(blocks, (0, 2, 1, 3)).reshape(agg_count, modes_count, 7 * modes_count)


def split_rows(coarse):
    agg_count, modes_count = coarse.shape[0], coarse.shape[1]
    blocks = jnp.transpose(coarse.reshape(agg_count, modes_count, 7, modes_count), (0, 2, 1, 3))
    return blocks[:, 0], blocks[:, 1:]


def smooth_coarse(coarse, modes, near_modes):
    own_block, lateral = split_rows(coarse)
    row_scale = jnp.sum(jnp.abs(coarse), axis=2) + EPSILON
    product = jnp.einsum("nij,njk->nik", own_block, modes, precision=HIGHEST)
    product = product + jnp.einsum("nfij,nfjk->nik", lateral, near_modes, precision=HIGHEST)
    return modes - OMEGA_COARSE * product / row_scale[:, :, None]


def galerkin_partials(coarse, smoothed, near_smoothed):
    own_block, lateral = split_rows(coarse)
    applied = jnp.einsum("nij,njl->nil", own_block, smoothed, precision=HIGHEST)
    centre = jnp.einsum("nik,nil->nkl", smoothed, applied, precision=HIGHEST)
    reached = jnp.einsum("nfij,nfjl->nfil", lateral, near_smoothed, precision=HIGHEST)
    face_terms = jnp.einsum("nik,nfil->nfkl", smoothed, reached, precision=HIGHEST)
    centre = centre + face_terms[:, 4] + face_terms[:, 5]
    return jnp.stack([centre, face_terms[:, 0], face_terms[:, 1], face_terms[:, 2], face_terms[:, 3]], axis=1)


def reference(near_modes, diag_blocks, face_blocks, face_rows, coarse_modes):
    grid_shape = near_modes.shape[:3]
    agg_count = grid_shape[0] * grid_shape[1] * grid_shape[2]

    def flatten(array_in):
        return array_in.reshape((agg_count,) + array_in.shape[3:])

    def ungrid(array_in):
        return array_in.reshape(grid_shape + array_in.shape[1:])

    near = flatten(neighbours(pad_grid(near_modes)))
    smoothed = smooth_fine(flatten(near_modes), near, flatten(diag_blocks), flatten(face_blocks), flatten(face_rows))
    near_smoothed = flatten(neighbours(pad_grid(ungrid(smoothed))))
    coarse_one = galerkin_fine(smoothed, near_smoothed, flatten(diag_blocks), flatten(face_blocks), flatten(face_rows))
    near_coarse = flatten(neighbours(pad_grid(coarse_modes)))
    coarse_smoothed = smooth_coarse(coarse_one, flatten(coarse_modes), near_coarse)
    near_coarse_smoothed = flatten(neighbours(pad_grid(ungrid(coarse_smoothed))))
    partials = galerkin_partials(coarse_one, coarse_smoothed, near_coarse_smoothed)
    columns = jnp.sum(ungrid(partials), axis=2)
    modes_count = coarse_modes.shape[3]
    coarse_two = jnp.transpose(columns, (0, 1, 3, 2, 4)).reshape(grid_shape[0], grid_shape[1], modes_count, 5 * modes_count)
    return ungrid(coarse_one), coarse_two
```

```python
import functools

import jax
import jax.numpy as jnp
from jax import lax
from jax.experimental import pallas as pl
from jax.experimental.pallas import tpu as pltpu
from jax.sharding import PartitionSpec as P

MESH = pl.DeviceIdType.MESH
HIGHEST = lax.Precision.HIGHEST
OMEGA_FINE = 2.0 / 3.0
OMEGA_COARSE = 1.0
EPSILON = 1e-06
LANES = 128


def dot_nt(left, right, precision=None):
    return lax.dot_general(
        left, right, (((1,), (1,)), ((), ())), precision=precision, preferred_element_type=jnp.float32
    )


def dot_nn(left, right, precision=None):
    return lax.dot_general(
        left, right, (((1,), (0,)), ((), ())), precision=precision, preferred_element_type=jnp.float32
    )


def split(value):
    high = value.astype(jnp.bfloat16).astype(jnp.float32)
    return jnp.concatenate([high, value - high], axis=0).astype(jnp.bfloat16)


def fold(value):
    half = value.shape[0] // 2
    return value[:half] + value[half:]


def split_into(source, high_ref, low_ref, rows, step):
    for start in range(0, rows, step):
        part = source[pl.ds(start, step)]
        high = part.astype(jnp.bfloat16)
        high_ref[pl.ds(start, step)] = high
        low_ref[pl.ds(start, step)] = (part - high.astype(jnp.float32)).astype(jnp.bfloat16)


def kernel(
    sizes,
    near_hbm,
    diag_hbm,
    face_hbm,
    rows_hbm,
    modes_hbm,
    coarse_out,
    column_out,
    near_x,
    near_y,
    near_z,
    smooth_x,
    smooth_y,
    smooth_z,
    diag_in,
    face_in,
    rows_in,
    modes_in,
    diag_high,
    diag_low,
    face_high,
    face_low,
    selector,
    product,
    diagonal,
    reach,
    own_block,
    modes_pack,
    modes_halo,
    right,
    left,
    part,
    gathered,
    load_sem,
    diag_sem,
    face_sem,
    near_send,
    near_recv,
    smooth_send,
    smooth_recv,
    modes_send,
    modes_recv,
    result_send,
    result_recv,
    sum_send,
    sum_recv,
):
    n_x, n_y, n_z = sizes
    count, modes, dofs = product.shape
    face = face_in.shape[2]
    last = count - 1
    gx, gy, gz = lax.axis_index("gx"), lax.axis_index("gy"), lax.axis_index("gz")
    has = [gx > 0, gx < n_x - 1, gy > 0, gy < n_y - 1, gz > 0, gz < n_z - 1]
    target = [
        {"gx": gx - 1},
        {"gx": gx + 1},
        {"gy": gy - 1},
        {"gy": gy + 1},
        {"gz": gz - 1},
        {"gz": gz + 1},
    ]
    passes_up = (gy == 2) & has[1]
    passes_down = (gy == 1) & has[0]
    pass_up = {"gx": gx + 1, "gy": gy - 1}
    pass_down = {"gx": gx - 1, "gy": gy + 1}
    peers = [lax.rem(gz + step, n_z) for step in range(1, n_z)]

    loads = [
        pltpu.make_async_copy(near_hbm.at[0, 0], near_z.at[pl.ds(1, count)], load_sem.at[0]),
        pltpu.make_async_copy(rows_hbm.at[0, 0], rows_in, load_sem.at[1]),
        pltpu.make_async_copy(modes_hbm.at[0, 0], modes_in, load_sem.at[2]),
    ]
    for load in loads:
        load.start()

    def load_diag(at):
        return pltpu.make_async_copy(diag_hbm.at[0, 0, at], diag_in.at[at], diag_sem.at[at])

    def load_face(at):
        return pltpu.make_async_copy(face_hbm.at[0, 0, at], face_in.at[at], face_sem.at[at])

    for at in range(count):
        load_diag(at).start()
    for at in range(count):
        load_face(at).start()

    right[...] = jnp.zeros_like(right)

    barrier = pltpu.get_barrier_semaphore()
    for side in range(4):

        @pl.when(has[side])
        def _(side=side):
            pl.semaphore_signal(barrier, inc=1, device_id=target[side], device_id_type=MESH)

    @pl.when(passes_up)
    def _():
        pl.semaphore_signal(barrier, inc=1, device_id=pass_up, device_id_type=MESH)

    @pl.when(passes_down)
    def _():
        pl.semaphore_signal(barrier, inc=1, device_id=pass_down, device_id_type=MESH)

    for peer in peers:
        pl.semaphore_signal(barrier, inc=1, device_id={"gz": peer}, device_id_type=MESH)

    for side in range(2):

        @pl.when(jnp.logical_not(has[side]))
        def _(side=side):
            near_x[side] = jnp.zeros_like(near_x[side])
            smooth_x[side] = jnp.zeros_like(smooth_x[side])

        @pl.when(jnp.logical_not(has[2 + side]))
        def _(side=side):
            near_y[side] = jnp.zeros_like(near_y[side])
            smooth_y[side] = jnp.zeros_like(smooth_y[side])

        @pl.when(jnp.logical_not(has[4 + side]))
        def _(side=side):
            near_z[side * (count + 1)] = jnp.zeros((modes, dofs), jnp.float32)
            smooth_z[side * (count + 1)] = jnp.zeros((modes, dofs), jnp.float32)

    for side in range(6):

        @pl.when(jnp.logical_not(has[side]))
        def _(side=side):
            modes_halo[side] = jnp.zeros_like(modes_halo[side])

    loads[2].wait()
    pieces = [modes_in[at].T for at in range(count)]
    pieces.append(jnp.zeros((modes, LANES - count * modes), jnp.float32))
    modes_pack[...] = jnp.concatenate(pieces, axis=1)
    loads[1].wait()

    def build_selector(at, carry):
        for side in range(6):
            chosen = rows_in[at, pl.ds(side, 1), :]
            for start in range(0, dofs, LANES):
                row = lax.broadcasted_iota(jnp.int32, (LANES, face), 0) + start
                hit = jnp.where(row == chosen, 1.0, 0.0).astype(jnp.bfloat16)
                selector[at, pl.ds(start, LANES), pl.ds(side * face, face)] = hit
        return carry

    lax.fori_loop(0, count, build_selector, 0)
    loads[0].wait()

    met = n_z - 1
    for flag in has[:4] + [passes_up | passes_down]:
        met = met + flag.astype(jnp.int32)
    pl.semaphore_wait(barrier, met)

    def halo(bufs, sems, side, at, landing):
        buf_x, buf_y, buf_z = bufs
        send, recv = sems
        if side < 2:
            dst = buf_x.at[landing, at]
        elif side < 4:
            dst = buf_y.at[landing - 2, at]
        else:
            dst = buf_z.at[(landing - 4) * (count + 1)]
        return pltpu.make_async_remote_copy(
            src_ref=buf_z.at[at + 1],
            dst_ref=dst,
            send_sem=send.at[side, at],
            recv_sem=recv.at[landing, at],
            device_id=target[side],
            device_id_type=MESH,
        )

    def passed(bufs, sems, up, at):
        buf_x, buf_y, _ = bufs
        send, recv = sems
        landing = 0 if up else 1
        return pltpu.make_async_remote_copy(
            src_ref=buf_y.at[landing, at],
            dst_ref=buf_x.at[landing, at],
            send_sem=send.at[6, at],
            recv_sem=recv.at[landing, at],
            device_id=pass_up if up else pass_down,
            device_id_type=MESH,
        )

    direct = [has[0] & (gy != 2), has[1] & (gy != 1), has[2], has[3], has[4], has[5]]

    def send_halo(bufs, sems, at):
        for side in (2, 3, 0, 1):

            @pl.when(direct[side])
            def _(side=side):
                halo(bufs, sems, side, at, side ^ 1).start()

        @pl.when(has[4] & (at == 0))
        def _():
            halo(bufs, sems, 4, at, 5).start()

        @pl.when(has[5] & (at == last))
        def _():
            halo(bufs, sems, 5, at, 4).start()

    def wait_y_and_pass(bufs, sems, at):
        for side in (2, 3):

            @pl.when(has[side])
            def _(side=side):
                halo(bufs, sems, side, at, side).wait_recv()

        @pl.when(passes_up)
        def _():
            passed(bufs, sems, True, at).start()

        @pl.when(passes_down)
        def _():
            passed(bufs, sems, False, at).start()

    def wait_xz(bufs, sems, at):
        for side in (0, 1):

            @pl.when(has[side])
            def _(side=side):
                halo(bufs, sems, side, at, side).wait_recv()

        @pl.when(has[4] & (at == 0))
        def _():
            halo(bufs, sems, 4, last, 4).wait_recv()

        @pl.when(has[5] & (at == last))
        def _():
            halo(bufs, sems, 5, 0, 5).wait_recv()

    def wait_sent(bufs, sems, at):
        for side in (2, 3, 0, 1):

            @pl.when(direct[side])
            def _(side=side):
                halo(bufs, sems, side, at, side ^ 1).wait_send()

        @pl.when(has[4] & (at == 0))
        def _():
            halo(bufs, sems, 4, at, 5).wait_send()

        @pl.when(has[5] & (at == last))
        def _():
            halo(bufs, sems, 5, at, 4).wait_send()

        @pl.when(passes_up)
        def _():
            passed(bufs, sems, True, at).wait_send()

        @pl.when(passes_down)
        def _():
            passed(bufs, sems, False, at).wait_send()

    near_bufs, near_sems = (near_x, near_y, near_z), (near_send, near_recv)
    smooth_bufs, smooth_sems = (smooth_x, smooth_y, smooth_z), (smooth_send, smooth_recv)

    def send_near(at, carry):
        send_halo(near_bufs, near_sems, at)
        return carry

    lax.fori_loop(0, count, send_near, 0)

    def modes_copy(side, landing):
        return pltpu.make_async_remote_copy(
            src_ref=modes_pack,
            dst_ref=modes_halo.at[landing],
            send_sem=modes_send.at[side],
            recv_sem=modes_recv.at[landing],
            device_id=target[side],
            device_id_type=MESH,
        )

    for side in range(6):

        @pl.when(has[side])
        def _(side=side):
            modes_copy(side, side ^ 1).start()

    def own_product(at, carry):
        load_diag(at).wait()
        split_into(diag_in.at[at], diag_high.at[at], diag_low.at[at], dofs, 64)
        here = []
        for start in range(0, dofs, LANES):
            block = diag_in[at, pl.ds(start, LANES), pl.ds(start, LANES)]
            row = lax.broadcasted_iota(jnp.int32, (LANES, LANES), 0)
            col = lax.broadcasted_iota(jnp.int32, (LANES, LANES), 1)
            here.append(jnp.sum(jnp.where(row == col, block, 0.0), axis=0, keepdims=True))
        diagonal[at] = jnp.concatenate(here, axis=1)
        value = split(near_z[at + 1])
        product[at] = fold(dot_nt(value, diag_high[at]) + dot_nt(value, diag_low[at]))
        return carry

    lax.fori_loop(0, count, own_product, 0)
    wait_y_and_pass(near_bufs, near_sems, 0)

    def smooth(at, carry):
        load_face(at).wait()
        for side in range(6):
            split_into(
                face_in.at[at, side], face_high.at[at, side], face_low.at[at, side], face, 64
            )
        wait_xz(near_bufs, near_sems, at)

        @pl.when(at < last)
        def _():
            wait_y_and_pass(near_bufs, near_sems, at + 1)

        terms = []
        for side in range(6):
            if side < 2:
                value = near_x[side, at]
            elif side < 4:
                value = near_y[side - 2, at]
            else:
                value = near_z[at + 2 * (side - 4)]
            value = split(value)
            terms.append(
                fold(dot_nt(value, face_high[at, side]) + dot_nt(value, face_low[at, side]))
            )
        terms = split(jnp.concatenate(terms, axis=1))
        total = product[at] + fold(dot_nt(terms, selector[at]))
        smooth_z[at + 1] = near_z[at + 1] - OMEGA_FINE * total / diagonal[at]
        send_halo(smooth_bufs, smooth_sems, at)

        @pl.when(at > 0)
        def _():
            wait_y_and_pass(smooth_bufs, smooth_sems, at - 1)

        return carry

    lax.fori_loop(0, count, smooth, 0)

    def coarse_local(at, carry):
        value = split(smooth_z[at + 1])
        applied = split(fold(dot_nt(value, diag_high[at]) + dot_nt(value, diag_low[at])))
        own = fold(dot_nt(value, applied))
        own_block[at] = own[:, :modes] + own[:, modes:]
        picked = dot_nn(value, selector[at]).astype(jnp.bfloat16)
        for side in range(6):
            here = picked[:, side * face : (side + 1) * face]
            reach[at, side] = split(
                fold(dot_nn(here, face_high[at, side]) + dot_nn(here, face_low[at, side]))
            )

        @pl.when(at == 1)
        def _():
            wait_y_and_pass(smooth_bufs, smooth_sems, last)

        return carry

    lax.fori_loop(0, count, coarse_local, 0)

    for side in range(6):

        @pl.when(has[side])
        def _(side=side):
            modes_copy(side, side).wait_recv()

    own_modes = modes_pack[...]
    zero_block = jnp.zeros((modes, modes), jnp.float32)

    def lane_block(value, at):
        return value[:, at * modes : (at + 1) * modes]

    along_z = (
        [lane_block(modes_halo[4], last)]
        + [lane_block(own_modes, at) for at in range(count)]
        + [lane_block(modes_halo[5], 0)]
    )
    around = []
    for at in range(count):
        sides = [lane_block(modes_halo[side], at) for side in range(4)]
        around.append(
            jnp.concatenate([along_z[at + 1]] + sides + [along_z[at], along_z[at + 2]], axis=1)
        )

    smoothed_t, through = [], []
    for at in range(count):
        wait_xz(smooth_bufs, smooth_sems, at)
        blocks = [own_block[at]]
        for side in range(6):
            if side < 2:
                value = smooth_x[side, at]
            elif side < 4:
                value = smooth_y[side - 2, at]
            else:
                value = smooth_z[at + 2 * (side - 4)]
            lateral = fold(dot_nt(reach[at, side], split(value)))
            blocks.append(lateral[:, :modes] + lateral[:, modes:])
        coarse = jnp.concatenate(blocks, axis=1)
        coarse_out[at] = coarse
        scale = dot_nt(jnp.ones_like(coarse), jnp.abs(coarse), HIGHEST) + EPSILON
        applied = dot_nt(around[at], coarse, HIGHEST)
        result = along_z[at + 1] - OMEGA_COARSE * applied / scale
        smoothed_t.append(result)
        through.append(dot_nn(result, coarse, HIGHEST))

    right_rows = [1, 2, 3, 4, 0, 0]
    filler = jnp.zeros((modes, LANES - count * modes), jnp.float32)
    right[pl.ds(0, modes), pl.ds(0, LANES)] = jnp.concatenate(smoothed_t + [filler], axis=1)

    def result_copy(side, landing):
        return pltpu.make_async_remote_copy(
            src_ref=right.at[pl.ds(0, modes), pl.ds(0, LANES)],
            dst_ref=right.at[
                pl.ds(right_rows[landing] * modes, modes), pl.ds((landing + 1) * LANES, LANES)
            ],
            send_sem=result_send.at[side],
            recv_sem=result_recv.at[landing],
            device_id=target[side],
            device_id_type=MESH,
        )

    for side in range(6):

        @pl.when(has[side])
        def _(side=side):
            result_copy(side, side ^ 1).start()

    def block_of(at, which):
        return lane_block(through[at], which)

    centre = []
    for at in range(count):
        value = block_of(at, 0)
        if at < last:
            value = value + block_of(at + 1, 5)
        if at > 0:
            value = value + block_of(at - 1, 6)
        centre.append(value)
    left[:, pl.ds(0, LANES)] = jnp.concatenate(centre + [filler], axis=1)
    for side in range(4):
        pieces = [block_of(at, side + 1) for at in range(count)]
        left[:, pl.ds((side + 1) * LANES, LANES)] = jnp.concatenate(pieces + [filler], axis=1)
    low = [zero_block] * last + [block_of(0, 5)]
    left[:, pl.ds(5 * LANES, LANES)] = jnp.concatenate(low + [filler], axis=1)
    high = [block_of(last, 6)] + [zero_block] * last
    left[:, pl.ds(6 * LANES, LANES)] = jnp.concatenate(high + [filler], axis=1)

    for side in range(6):

        @pl.when(has[side])
        def _(side=side):
            result_copy(side, side).wait_recv()

    part[...] = dot_nt(left[...], right[...], HIGHEST)
    gathered[gz] = part[...]
    shares = [
        pltpu.make_async_remote_copy(
            src_ref=part,
            dst_ref=gathered.at[gz],
            send_sem=sum_send.at[at],
            recv_sem=sum_recv.at[at],
            device_id={"gz": peer},
            device_id_type=MESH,
        )
        for at, peer in enumerate(peers)
    ]
    for share in shares:
        share.start()

    def finish(at, carry):
        wait_sent(near_bufs, near_sems, at)
        wait_sent(smooth_bufs, smooth_sems, at)
        return carry

    lax.fori_loop(0, count, finish, 0)
    for side in range(6):

        @pl.when(has[side])
        def _(side=side):
            modes_copy(side, side ^ 1).wait_send()
            result_copy(side, side ^ 1).wait_send()

    for share in shares:
        share.wait()
    total = gathered[0]
    for at in range(1, n_z):
        total = total + gathered[at]
    column_out[...] = total[:, : 5 * modes]


def per_device(sizes, near_modes, diag_blocks, face_blocks, face_rows, coarse_modes):
    count, modes, dofs = near_modes.shape[2:]
    face = face_blocks.shape[4]
    n_z = sizes[2]
    any_space = pl.BlockSpec(memory_space=pl.ANY)
    vmem = pl.BlockSpec(memory_space=pltpu.VMEM)
    f32, bf16 = jnp.float32, jnp.bfloat16
    dma = pltpu.SemaphoreType.DMA
    coarse_one, column = pl.pallas_call(
        functools.partial(kernel, sizes),
        out_shape=(
            jax.ShapeDtypeStruct((count, modes, 7 * modes), f32),
            jax.ShapeDtypeStruct((modes, 5 * modes), f32),
        ),
        in_specs=[any_space] * 5,
        out_specs=(vmem, vmem),
        scratch_shapes=[
            pltpu.VMEM((2, count, modes, dofs), f32),
            pltpu.VMEM((2, count, modes, dofs), f32),
            pltpu.VMEM((count + 2, modes, dofs), f32),
            pltpu.VMEM((2, count, modes, dofs), f32),
            pltpu.VMEM((2, count, modes, dofs), f32),
            pltpu.VMEM((count + 2, modes, dofs), f32),
            pltpu.VMEM((count, dofs, dofs), f32),
            pltpu.VMEM((count, 6, face, dofs), f32),
            pltpu.VMEM((count, 6, face), jnp.int32),
            pltpu.VMEM((count, modes, modes), f32),
            pltpu.VMEM((count, dofs, dofs), bf16),
            pltpu.VMEM((count, dofs, dofs), bf16),
            pltpu.VMEM((count, 6, face, dofs), bf16),
            pltpu.VMEM((count, 6, face, dofs), bf16),
            pltpu.VMEM((count, dofs, 6 * face), bf16),
            pltpu.VMEM((count, modes, dofs), f32),
            pltpu.VMEM((count, 1, dofs), f32),
            pltpu.VMEM((count, 6, 2 * modes, dofs), bf16),
            pltpu.VMEM((count, modes, modes), f32),
            pltpu.VMEM((modes, LANES), f32),
            pltpu.VMEM((6, modes, LANES), f32),
            pltpu.VMEM((LANES, 7 * LANES), f32),
            pltpu.VMEM((modes, 7 * LANES), f32),
            pltpu.VMEM((modes, LANES), f32),
            pltpu.VMEM((n_z, modes, LANES), f32),
            dma((3,)),
            dma((count,)),
            dma((count,)),
            dma((7, count)),
            dma((6, count)),
            dma((7, count)),
            dma((6, count)),
            dma((6,)),
            dma((6,)),
            dma((6,)),
            dma((6,)),
            dma((n_z - 1,)),
            dma((n_z - 1,)),
        ],
        compiler_params=pltpu.CompilerParams(
            collective_id=0, has_side_effects=True, vmem_limit_bytes=48 * 2**20
        ),
        cost_estimate=pl.CostEstimate(flops=2 * 10**9, bytes_accessed=11 * 10**6, transcendentals=0),
    )(near_modes, diag_blocks, face_blocks, face_rows, coarse_modes)
    return coarse_one[None, None], column[None, None]


def solution(mesh):
    placed = (
        P("gx", "gy", "gz", None, None),
        P("gx", "gy", "gz", None, None),
        P("gx", "gy", "gz", None, None, None),
        P("gx", "gy", "gz", None, None),
        P("gx", "gy", "gz", None, None),
    )
    sizes = tuple(mesh.shape[axis] for axis in ("gx", "gy", "gz"))
    return jax.shard_map(
        functools.partial(per_device, sizes),
        mesh=mesh,
        in_specs=placed,
        out_specs=(P("gx", "gy", "gz", None, None), P("gx", "gy", None, None)),
        check_vma=False,
    )
```

```python
import functools

import jax
import jax.numpy as jnp
from jax import lax
from jax.experimental import pallas as pl
from jax.experimental.pallas import tpu as pltpu
from jax.sharding import PartitionSpec as P

MESH = pl.DeviceIdType.MESH
HIGHEST = lax.Precision.HIGHEST
OMEGA_FINE = 2.0 / 3.0
OMEGA_COARSE = 1.0
EPSILON = 1e-06
LANES = 128


def dot_nt(left, right, precision=None):
    return lax.dot_general(
        left, right, (((1,), (1,)), ((), ())), precision=precision, preferred_element_type=jnp.float32
    )


def dot_nn(left, right, precision=None):
    return lax.dot_general(
        left, right, (((1,), (0,)), ((), ())), precision=precision, preferred_element_type=jnp.float32
    )


def split(value):
    high = value.astype(jnp.bfloat16).astype(jnp.float32)
    return jnp.concatenate([high, value - high], axis=0).astype(jnp.bfloat16)


def fold(value):
    half = value.shape[0] // 2
    return value[:half] + value[half:]


def split_into(source, high_ref, low_ref, rows, step):
    for start in range(0, rows, step):
        part = source[pl.ds(start, step)]
        high = part.astype(jnp.bfloat16)
        high_ref[pl.ds(start, step)] = high
        low_ref[pl.ds(start, step)] = (part - high.astype(jnp.float32)).astype(jnp.bfloat16)


def kernel(
    sizes,
    near_hbm,
    diag_hbm,
    face_hbm,
    rows_hbm,
    modes_hbm,
    coarse_out,
    column_out,
    near_x,
    near_y,
    near_z,
    smooth_x,
    smooth_y,
    smooth_z,
    diag_in,
    face_in,
    rows_in,
    modes_in,
    diag_high,
    diag_low,
    face_high,
    face_low,
    selector,
    product,
    diagonal,
    reach,
    own_block,
    modes_pack,
    modes_halo,
    right,
    left,
    part,
    gathered,
    load_sem,
    diag_sem,
    face_sem,
    near_send,
    near_recv,
    smooth_send,
    smooth_recv,
    modes_send,
    modes_recv,
    result_send,
    result_recv,
    sum_send,
    sum_recv,
):
    n_x, n_y, n_z = sizes
    count, modes, dofs = product.shape
    face = face_in.shape[2]
    last = count - 1
    gx, gy, gz = lax.axis_index("gx"), lax.axis_index("gy"), lax.axis_index("gz")
    has = [gx > 0, gx < n_x - 1, gy > 0, gy < n_y - 1, gz > 0, gz < n_z - 1]
    target = [
        {"gx": gx - 1},
        {"gx": gx + 1},
        {"gy": gy - 1},
        {"gy": gy + 1},
        {"gz": gz - 1},
        {"gz": gz + 1},
    ]
    peers = [lax.rem(gz + step, n_z) for step in range(1, n_z)]

    loads = [
        pltpu.make_async_copy(near_hbm.at[0, 0], near_z.at[pl.ds(1, count)], load_sem.at[0]),
        pltpu.make_async_copy(rows_hbm.at[0, 0], rows_in, load_sem.at[1]),
        pltpu.make_async_copy(modes_hbm.at[0, 0], modes_in, load_sem.at[2]),
    ]
    for load in loads:
        load.start()

    def load_diag(at):
        return pltpu.make_async_copy(diag_hbm.at[0, 0, at], diag_in.at[at], diag_sem.at[at])

    def load_face(at):
        return pltpu.make_async_copy(face_hbm.at[0, 0, at], face_in.at[at], face_sem.at[at])

    for at in range(count):
        load_diag(at).start()
    for at in range(count):
        load_face(at).start()

    right[...] = jnp.zeros_like(right)

    barrier = pltpu.get_barrier_semaphore()
    for side in range(4):

        @pl.when(has[side])
        def _(side=side):
            pl.semaphore_signal(barrier, inc=1, device_id=target[side], device_id_type=MESH)

    for peer in peers:
        pl.semaphore_signal(barrier, inc=1, device_id={"gz": peer}, device_id_type=MESH)

    for side in range(2):

        @pl.when(jnp.logical_not(has[side]))
        def _(side=side):
            near_x[side] = jnp.zeros_like(near_x[side])
            smooth_x[side] = jnp.zeros_like(smooth_x[side])

        @pl.when(jnp.logical_not(has[2 + side]))
        def _(side=side):
            near_y[side] = jnp.zeros_like(near_y[side])
            smooth_y[side] = jnp.zeros_like(smooth_y[side])

        @pl.when(jnp.logical_not(has[4 + side]))
        def _(side=side):
            near_z[side * (count + 1)] = jnp.zeros((modes, dofs), jnp.float32)
            smooth_z[side * (count + 1)] = jnp.zeros((modes, dofs), jnp.float32)

    for side in range(6):

        @pl.when(jnp.logical_not(has[side]))
        def _(side=side):
            modes_halo[side] = jnp.zeros_like(modes_halo[side])

    loads[2].wait()
    pieces = [modes_in[at].T for at in range(count)]
    pieces.append(jnp.zeros((modes, LANES - count * modes), jnp.float32))
    modes_pack[...] = jnp.concatenate(pieces, axis=1)
    loads[1].wait()

    def build_selector(at, carry):
        for side in range(6):
            chosen = rows_in[side, pl.ds(at, 1), :]
            for start in range(0, dofs, LANES):
                row = lax.broadcasted_iota(jnp.int32, (LANES, face), 0) + start
                hit = jnp.where(row == chosen, 1.0, 0.0).astype(jnp.bfloat16)
                selector[at, pl.ds(start, LANES), pl.ds(side * face, face)] = hit
        return carry

    lax.fori_loop(0, count, build_selector, 0)
    loads[0].wait()

    met = n_z - 1
    for flag in has[:4]:
        met = met + flag.astype(jnp.int32)
    pl.semaphore_wait(barrier, met)

    def halo(bufs, sems, side, at, landing):
        buf_x, buf_y, buf_z = bufs
        send, recv = sems
        if side < 2:
            dst = buf_x.at[landing, at]
        elif side < 4:
            dst = buf_y.at[landing - 2, at]
        else:
            dst = buf_z.at[(landing - 4) * (count + 1)]
        return pltpu.make_async_remote_copy(
            src_ref=buf_z.at[at + 1],
            dst_ref=dst,
            send_sem=send.at[side, at],
            recv_sem=recv.at[landing, at],
            device_id=target[side],
            device_id_type=MESH,
        )

    def send_halo(bufs, sems, at):
        for side in (2, 3, 0, 1):

            @pl.when(has[side])
            def _(side=side):
                halo(bufs, sems, side, at, side ^ 1).start()

        @pl.when(has[4] & (at == 0))
        def _():
            halo(bufs, sems, 4, at, 5).start()

        @pl.when(has[5] & (at == last))
        def _():
            halo(bufs, sems, 5, at, 4).start()

    def wait_y(bufs, sems, at):
        for side in (2, 3):

            @pl.when(has[side])
            def _(side=side):
                halo(bufs, sems, side, at, side).wait_recv()

    def wait_xz(bufs, sems, at):
        for side in (0, 1):

            @pl.when(has[side])
            def _(side=side):
                halo(bufs, sems, side, at, side).wait_recv()

        @pl.when(has[4] & (at == 0))
        def _():
            halo(bufs, sems, 4, last, 4).wait_recv()

        @pl.when(has[5] & (at == last))
        def _():
            halo(bufs, sems, 5, 0, 5).wait_recv()

    def wait_sent(bufs, sems, at):
        for side in (2, 3, 0, 1):

            @pl.when(has[side])
            def _(side=side):
                halo(bufs, sems, side, at, side ^ 1).wait_send()

        @pl.when(has[4] & (at == 0))
        def _():
            halo(bufs, sems, 4, at, 5).wait_send()

        @pl.when(has[5] & (at == last))
        def _():
            halo(bufs, sems, 5, at, 4).wait_send()

    near_bufs, near_sems = (near_x, near_y, near_z), (near_send, near_recv)
    smooth_bufs, smooth_sems = (smooth_x, smooth_y, smooth_z), (smooth_send, smooth_recv)

    def send_near(at, carry):
        send_halo(near_bufs, near_sems, at)
        return carry

    lax.fori_loop(0, count, send_near, 0)

    def modes_copy(side, landing):
        return pltpu.make_async_remote_copy(
            src_ref=modes_pack,
            dst_ref=modes_halo.at[landing],
            send_sem=modes_send.at[side],
            recv_sem=modes_recv.at[landing],
            device_id=target[side],
            device_id_type=MESH,
        )

    for side in range(6):

        @pl.when(has[side])
        def _(side=side):
            modes_copy(side, side ^ 1).start()

    def own_product(at, carry):
        load_diag(at).wait()
        split_into(diag_in.at[at], diag_high.at[at], diag_low.at[at], dofs, 64)
        here = []
        for start in range(0, dofs, LANES):
            block = diag_in[at, pl.ds(start, LANES), pl.ds(start, LANES)]
            row = lax.broadcasted_iota(jnp.int32, (LANES, LANES), 0)
            col = lax.broadcasted_iota(jnp.int32, (LANES, LANES), 1)
            here.append(jnp.sum(jnp.where(row == col, block, 0.0), axis=0, keepdims=True))
        diagonal[at] = jnp.concatenate(here, axis=1)
        value = split(near_z[at + 1])
        product[at] = fold(dot_nt(value, diag_high[at]) + dot_nt(value, diag_low[at]))
        return carry

    lax.fori_loop(0, count, own_product, 0)

    def smooth(at, carry):
        load_face(at).wait()
        for side in range(6):
            split_into(
                face_in.at[at, side], face_high.at[at, side], face_low.at[at, side], face, 64
            )
        wait_y(near_bufs, near_sems, at)
        wait_xz(near_bufs, near_sems, at)

        terms = []
        for side in range(6):
            if side < 2:
                value = near_x[side, at]
            elif side < 4:
                value = near_y[side - 2, at]
            else:
                value = near_z[at + 2 * (side - 4)]
            value = split(value)
            terms.append(
                fold(dot_nt(value, face_high[at, side]) + dot_nt(value, face_low[at, side]))
            )
        terms = split(jnp.concatenate(terms, axis=1))
        total = product[at] + fold(dot_nt(terms, selector[at]))
        smooth_z[at + 1] = near_z[at + 1] - OMEGA_FINE * total / diagonal[at]
        send_halo(smooth_bufs, smooth_sems, at)
        return carry

    lax.fori_loop(0, count, smooth, 0)

    def coarse_local(at, carry):
        value = split(smooth_z[at + 1])
        applied = split(fold(dot_nt(value, diag_high[at]) + dot_nt(value, diag_low[at])))
        own = fold(dot_nt(value, applied))
        own_block[at] = own[:, :modes] + own[:, modes:]
        picked = dot_nn(value, selector[at]).astype(jnp.bfloat16)
        for side in range(6):
            here = picked[:, side * face : (side + 1) * face]
            reach[at, side] = split(
                fold(dot_nn(here, face_high[at, side]) + dot_nn(here, face_low[at, side]))
            )
        return carry

    lax.fori_loop(0, count, coarse_local, 0)

    for side in range(6):

        @pl.when(has[side])
        def _(side=side):
            modes_copy(side, side).wait_recv()

    own_modes = modes_pack[...]
    zero_block = jnp.zeros((modes, modes), jnp.float32)

    def lane_block(value, at):
        return value[:, at * modes : (at + 1) * modes]

    along_z = (
        [lane_block(modes_halo[4], last)]
        + [lane_block(own_modes, at) for at in range(count)]
        + [lane_block(modes_halo[5], 0)]
    )
    around = []
    for at in range(count):
        sides = [lane_block(modes_halo[side], at) for side in range(4)]
        around.append(
            jnp.concatenate([along_z[at + 1]] + sides + [along_z[at], along_z[at + 2]], axis=1)
        )

    smoothed_t, through = [], []
    for at in range(count):
        wait_y(smooth_bufs, smooth_sems, at)
        wait_xz(smooth_bufs, smooth_sems, at)
        blocks = [own_block[at]]
        for side in range(6):
            if side < 2:
                value = smooth_x[side, at]
            elif side < 4:
                value = smooth_y[side - 2, at]
            else:
                value = smooth_z[at + 2 * (side - 4)]
            lateral = fold(dot_nt(reach[at, side], split(value)))
            blocks.append(lateral[:, :modes] + lateral[:, modes:])
        coarse = jnp.concatenate(blocks, axis=1)
        coarse_out[at] = coarse
        scale = dot_nt(jnp.ones_like(coarse), jnp.abs(coarse), HIGHEST) + EPSILON
        applied = dot_nt(around[at], coarse, HIGHEST)
        result = along_z[at + 1] - OMEGA_COARSE * applied / scale
        smoothed_t.append(result)
        through.append(dot_nn(result, coarse, HIGHEST))

    right_rows = [1, 2, 3, 4, 0, 0]
    filler = jnp.zeros((modes, LANES - count * modes), jnp.float32)
    right[pl.ds(0, modes), pl.ds(0, LANES)] = jnp.concatenate(smoothed_t + [filler], axis=1)

    def result_copy(side, landing):
        return pltpu.make_async_remote_copy(
            src_ref=right.at[pl.ds(0, modes), pl.ds(0, LANES)],
            dst_ref=right.at[
                pl.ds(right_rows[landing] * modes, modes), pl.ds((landing + 1) * LANES, LANES)
            ],
            send_sem=result_send.at[side],
            recv_sem=result_recv.at[landing],
            device_id=target[side],
            device_id_type=MESH,
        )

    for side in range(6):

        @pl.when(has[side])
        def _(side=side):
            result_copy(side, side ^ 1).start()

    def block_of(at, which):
        return lane_block(through[at], which)

    centre = []
    for at in range(count):
        value = block_of(at, 0)
        if at < last:
            value = value + block_of(at + 1, 5)
        if at > 0:
            value = value + block_of(at - 1, 6)
        centre.append(value)
    left[:, pl.ds(0, LANES)] = jnp.concatenate(centre + [filler], axis=1)
    for side in range(4):
        pieces = [block_of(at, side + 1) for at in range(count)]
        left[:, pl.ds((side + 1) * LANES, LANES)] = jnp.concatenate(pieces + [filler], axis=1)
    low = [zero_block] * last + [block_of(0, 5)]
    left[:, pl.ds(5 * LANES, LANES)] = jnp.concatenate(low + [filler], axis=1)
    high = [block_of(last, 6)] + [zero_block] * last
    left[:, pl.ds(6 * LANES, LANES)] = jnp.concatenate(high + [filler], axis=1)

    for side in range(6):

        @pl.when(has[side])
        def _(side=side):
            result_copy(side, side).wait_recv()

    part[...] = dot_nt(left[...], right[...], HIGHEST)
    gathered[gz] = part[...]
    shares = [
        pltpu.make_async_remote_copy(
            src_ref=part,
            dst_ref=gathered.at[gz],
            send_sem=sum_send.at[at],
            recv_sem=sum_recv.at[at],
            device_id={"gz": peer},
            device_id_type=MESH,
        )
        for at, peer in enumerate(peers)
    ]
    for share in shares:
        share.start()

    def finish(at, carry):
        wait_sent(near_bufs, near_sems, at)
        wait_sent(smooth_bufs, smooth_sems, at)
        return carry

    lax.fori_loop(0, count, finish, 0)
    for side in range(6):

        @pl.when(has[side])
        def _(side=side):
            modes_copy(side, side ^ 1).wait_send()
            result_copy(side, side ^ 1).wait_send()

    for share in shares:
        share.wait()
    total = gathered[0]
    for at in range(1, n_z):
        total = total + gathered[at]
    column_out[...] = total[:, : 5 * modes]


def per_device(sizes, near_modes, diag_blocks, face_blocks, face_rows, coarse_modes):
    count, modes, dofs = near_modes.shape[2:]
    face = face_blocks.shape[4]
    n_z = sizes[2]
    any_space = pl.BlockSpec(memory_space=pltpu.HBM)
    vmem = pl.BlockSpec(memory_space=pltpu.VMEM)
    f32, bf16 = jnp.float32, jnp.bfloat16
    dma = pltpu.SemaphoreType.DMA
    coarse_one, column = pl.pallas_call(
        functools.partial(kernel, sizes),
        out_shape=(
            jax.ShapeDtypeStruct((count, modes, 7 * modes), f32),
            jax.ShapeDtypeStruct((modes, 5 * modes), f32),
        ),
        in_specs=[any_space] * 5,
        out_specs=(vmem, vmem),
        scratch_shapes=[
            pltpu.VMEM((2, count, modes, dofs), f32),
            pltpu.VMEM((2, count, modes, dofs), f32),
            pltpu.VMEM((count + 2, modes, dofs), f32),
            pltpu.VMEM((2, count, modes, dofs), f32),
            pltpu.VMEM((2, count, modes, dofs), f32),
            pltpu.VMEM((count + 2, modes, dofs), f32),
            pltpu.VMEM((count, dofs, dofs), f32),
            pltpu.VMEM((count, 6, face, dofs), f32),
            pltpu.VMEM((6, count, face), jnp.int32),
            pltpu.VMEM((count, modes, modes), f32),
            pltpu.VMEM((count, dofs, dofs), bf16),
            pltpu.VMEM((count, dofs, dofs), bf16),
            pltpu.VMEM((count, 6, face, dofs), bf16),
            pltpu.VMEM((count, 6, face, dofs), bf16),
            pltpu.VMEM((count, dofs, 6 * face), bf16),
            pltpu.VMEM((count, modes, dofs), f32),
            pltpu.VMEM((count, 1, dofs), f32),
            pltpu.VMEM((count, 6, 2 * modes, dofs), bf16),
            pltpu.VMEM((count, modes, modes), f32),
            pltpu.VMEM((modes, LANES), f32),
            pltpu.VMEM((6, modes, LANES), f32),
            pltpu.VMEM((LANES, 7 * LANES), f32),
            pltpu.VMEM((modes, 7 * LANES), f32),
            pltpu.VMEM((modes, LANES), f32),
            pltpu.VMEM((n_z, modes, LANES), f32),
            dma((3,)),
            dma((count,)),
            dma((count,)),
            dma((6, count)),
            dma((6, count)),
            dma((6, count)),
            dma((6, count)),
            dma((6,)),
            dma((6,)),
            dma((6,)),
            dma((6,)),
            dma((n_z - 1,)),
            dma((n_z - 1,)),
        ],
        compiler_params=pltpu.CompilerParams(
            collective_id=0, has_side_effects=True, vmem_limit_bytes=2**26 - 10550 * 1024
        ),
        cost_estimate=pl.CostEstimate(flops=2 * 10**9, bytes_accessed=11 * 10**6, transcendentals=0),
    )(near_modes, diag_blocks, face_blocks, jnp.transpose(face_rows, (0, 1, 3, 2, 4)), coarse_modes)
    return coarse_one[None, None], column[None, None]


def solution(mesh):
    placed = (
        P("gx", "gy", "gz", None, None),
        P("gx", "gy", "gz", None, None),
        P("gx", "gy", "gz", None, None, None),
        P("gx", "gy", "gz", None, None),
        P("gx", "gy", "gz", None, None),
    )
    sizes = tuple(mesh.shape[axis] for axis in ("gx", "gy", "gz"))
    return jax.shard_map(
        functools.partial(per_device, sizes),
        mesh=mesh,
        in_specs=placed,
        out_specs=(P("gx", "gy", "gz", None, None), P("gx", "gy", None, None)),
        check_vma=False,
    )
```

```python
import functools

import jax
import jax.numpy as jnp
from jax import lax
from jax.experimental import pallas as pl
from jax.experimental.pallas import tpu as pltpu
from jax.sharding import PartitionSpec as P

MESH = pl.DeviceIdType.MESH
OMEGA_FINE = 2.0 / 3.0
OMEGA_COARSE = 1.0
EPSILON = 1e-06
LANES = 128


def dot_nt(left, right, precision=None):
    return lax.dot_general(
        left, right, (((1,), (1,)), ((), ())), precision=precision, preferred_element_type=jnp.float32
    )


def dot_nn(left, right, precision=None):
    return lax.dot_general(
        left, right, (((1,), (0,)), ((), ())), precision=precision, preferred_element_type=jnp.float32
    )


def split(value):
    high = value.astype(jnp.bfloat16).astype(jnp.float32)
    return jnp.concatenate([high, value - high], axis=0).astype(jnp.bfloat16)


def two_pieces(value):
    high = value.astype(jnp.bfloat16)
    return high, (value - high.astype(jnp.float32)).astype(jnp.bfloat16)


def product_of(dot, left, right):
    return fold(dot(left, right[0]) + dot(left, right[1]))


def fold(value):
    half = value.shape[0] // 2
    return value[:half] + value[half:]


def split_into(source, high_ref, low_ref, rows, step):
    for start in range(0, rows, step):
        part = source[pl.ds(start, step)]
        high = part.astype(jnp.bfloat16)
        high_ref[pl.ds(start, step)] = high
        low_ref[pl.ds(start, step)] = (part - high.astype(jnp.float32)).astype(jnp.bfloat16)


def kernel(
    sizes,
    near_hbm,
    diag_hbm,
    face_hbm,
    rows_hbm,
    modes_hbm,
    coarse_out,
    column_out,
    near_x,
    near_y,
    near_z,
    smooth_x,
    smooth_y,
    smooth_z,
    diag_in,
    face_in,
    rows_in,
    modes_in,
    diag_high,
    diag_low,
    face_high,
    face_low,
    selector,
    product,
    diagonal,
    reach,
    own_block,
    modes_pack,
    modes_halo,
    right,
    left,
    part,
    gathered,
    load_sem,
    diag_sem,
    face_sem,
    near_send,
    near_recv,
    smooth_send,
    smooth_recv,
    modes_send,
    modes_recv,
    result_send,
    result_recv,
    sum_send,
    sum_recv,
):
    n_x, n_y, n_z = sizes
    count, modes, dofs = product.shape
    face = face_in.shape[2]
    last = count - 1
    gx, gy, gz = lax.axis_index("gx"), lax.axis_index("gy"), lax.axis_index("gz")
    has = [gx > 0, gx < n_x - 1, gy > 0, gy < n_y - 1, gz > 0, gz < n_z - 1]
    target = [
        {"gx": gx - 1},
        {"gx": gx + 1},
        {"gy": gy - 1},
        {"gy": gy + 1},
        {"gz": gz - 1},
        {"gz": gz + 1},
    ]
    peers = [lax.rem(gz + step, n_z) for step in range(1, n_z)]

    loads = [
        pltpu.make_async_copy(near_hbm.at[0, 0], near_z.at[pl.ds(1, count)], load_sem.at[0]),
        pltpu.make_async_copy(rows_hbm.at[0, 0], rows_in, load_sem.at[1]),
        pltpu.make_async_copy(modes_hbm.at[0, 0], modes_in, load_sem.at[2]),
    ]
    for load in loads:
        load.start()

    def load_diag(at):
        return pltpu.make_async_copy(diag_hbm.at[0, 0, at], diag_in.at[at], diag_sem.at[at])

    def load_face(at):
        return pltpu.make_async_copy(face_hbm.at[0, 0, at], face_in.at[at], face_sem.at[at])

    for at in range(count):
        load_diag(at).start()
    for at in range(count):
        load_face(at).start()

    right[...] = jnp.zeros_like(right)

    barrier = pltpu.get_barrier_semaphore()
    for side in range(4):

        @pl.when(has[side])
        def _(side=side):
            pl.semaphore_signal(barrier, inc=1, device_id=target[side], device_id_type=MESH)

    for peer in peers:
        pl.semaphore_signal(barrier, inc=1, device_id={"gz": peer}, device_id_type=MESH)

    for side in range(2):

        @pl.when(jnp.logical_not(has[side]))
        def _(side=side):
            near_x[side] = jnp.zeros_like(near_x[side])
            smooth_x[side] = jnp.zeros_like(smooth_x[side])

        @pl.when(jnp.logical_not(has[2 + side]))
        def _(side=side):
            near_y[side] = jnp.zeros_like(near_y[side])
            smooth_y[side] = jnp.zeros_like(smooth_y[side])

        @pl.when(jnp.logical_not(has[4 + side]))
        def _(side=side):
            near_z[side * (count + 1)] = jnp.zeros((modes, dofs), jnp.float32)
            smooth_z[side * (count + 1)] = jnp.zeros((modes, dofs), jnp.float32)

    for side in range(6):

        @pl.when(jnp.logical_not(has[side]))
        def _(side=side):
            modes_halo[side] = jnp.zeros_like(modes_halo[side])

    loads[0].wait()

    met = n_z - 1
    for flag in has[:4]:
        met = met + flag.astype(jnp.int32)
    pl.semaphore_wait(barrier, met)

    def halo(bufs, sems, side, at, landing):
        buf_x, buf_y, buf_z = bufs
        send, recv = sems
        if side < 2:
            dst = buf_x.at[landing, at]
        elif side < 4:
            dst = buf_y.at[landing - 2, at]
        else:
            dst = buf_z.at[(landing - 4) * (count + 1)]
        return pltpu.make_async_remote_copy(
            src_ref=buf_z.at[at + 1],
            dst_ref=dst,
            send_sem=send.at[side, at],
            recv_sem=recv.at[landing, at],
            device_id=target[side],
            device_id_type=MESH,
        )

    def send_halo(bufs, sems, at):
        for side in (0, 1, 2, 3):

            @pl.when(has[side])
            def _(side=side):
                halo(bufs, sems, side, at, side ^ 1).start()

    def send_z_low(bufs, sems):
        @pl.when(has[4])
        def _():
            halo(bufs, sems, 4, 0, 5).start()

    def send_z_high(bufs, sems):
        @pl.when(has[5])
        def _():
            halo(bufs, sems, 5, last, 4).start()

    def wait_y(bufs, sems, at):
        for side in (2, 3):

            @pl.when(has[side])
            def _(side=side):
                halo(bufs, sems, side, at, side).wait_recv()

    def wait_xz(bufs, sems, at):
        for side in (0, 1):

            @pl.when(has[side])
            def _(side=side):
                halo(bufs, sems, side, at, side).wait_recv()

        @pl.when(has[4] & (at == 0))
        def _():
            halo(bufs, sems, 4, last, 4).wait_recv()

        @pl.when(has[5] & (at == last))
        def _():
            halo(bufs, sems, 5, 0, 5).wait_recv()

    def wait_sent(bufs, sems, at):
        for side in (0, 1, 2, 3):

            @pl.when(has[side])
            def _(side=side):
                halo(bufs, sems, side, at, side ^ 1).wait_send()


    def wait_sent_z(bufs, sems):
        @pl.when(has[4])
        def _():
            halo(bufs, sems, 4, 0, 5).wait_send()

        @pl.when(has[5])
        def _():
            halo(bufs, sems, 5, last, 4).wait_send()

    near_bufs, near_sems = (near_x, near_y, near_z), (near_send, near_recv)
    smooth_bufs, smooth_sems = (smooth_x, smooth_y, smooth_z), (smooth_send, smooth_recv)

    def send_near(at, carry):
        send_halo(near_bufs, near_sems, at)
        return carry

    lax.fori_loop(0, count, send_near, 0)
    send_z_low(near_bufs, near_sems)
    send_z_high(near_bufs, near_sems)

    loads[2].wait()
    pieces = [modes_in[at].T for at in range(count)]
    pieces.append(jnp.zeros((modes, LANES - count * modes), jnp.float32))
    modes_pack[...] = jnp.concatenate(pieces, axis=1)
    def modes_copy(side, landing):
        return pltpu.make_async_remote_copy(
            src_ref=modes_pack,
            dst_ref=modes_halo.at[landing],
            send_sem=modes_send.at[side],
            recv_sem=modes_recv.at[landing],
            device_id=target[side],
            device_id_type=MESH,
        )

    for side in range(6):

        @pl.when(has[side])
        def _(side=side):
            modes_copy(side, side ^ 1).start()

    loads[1].wait()

    def build_selector(at, carry):
        for side in range(6):
            chosen = rows_in[side, pl.ds(at, 1), :]
            for start in range(0, dofs, LANES):
                row = lax.broadcasted_iota(jnp.int32, (LANES, face), 0) + start
                hit = jnp.where(row == chosen, 1.0, 0.0).astype(jnp.bfloat16)
                selector[at, pl.ds(start, LANES), pl.ds(side * face, face)] = hit
        return carry

    lax.fori_loop(0, count, build_selector, 0)
    def own_product(at, carry):
        load_diag(at).wait()
        split_into(diag_in.at[at], diag_high.at[at], diag_low.at[at], dofs, 64)
        here = []
        for start in range(0, dofs, LANES):
            block = diag_in[at, pl.ds(start, LANES), pl.ds(start, LANES)]
            row = lax.broadcasted_iota(jnp.int32, (LANES, LANES), 0)
            col = lax.broadcasted_iota(jnp.int32, (LANES, LANES), 1)
            here.append(jnp.sum(jnp.where(row == col, block, 0.0), axis=0, keepdims=True))
        diagonal[at] = jnp.concatenate(here, axis=1)
        value = split(near_z[at + 1])
        product[at] = fold(dot_nt(value, diag_high[at]) + dot_nt(value, diag_low[at]))
        return carry

    lax.fori_loop(0, count, own_product, 0)

    def split_faces(at, carry):
        load_face(at).wait()
        for side in range(6):
            split_into(
                face_in.at[at, side], face_high.at[at, side], face_low.at[at, side], face, 64
            )
        return carry

    lax.fori_loop(0, count, split_faces, 0)

    def smooth(at, carry):
        wait_y(near_bufs, near_sems, at)
        wait_xz(near_bufs, near_sems, at)

        terms = []
        for side in range(6):
            if side < 2:
                value = near_x[side, at]
            elif side < 4:
                value = near_y[side - 2, at]
            else:
                value = near_z[at + 2 * (side - 4)]
            value = split(value)
            terms.append(
                fold(dot_nt(value, face_high[at, side]) + dot_nt(value, face_low[at, side]))
            )
        terms = split(jnp.concatenate(terms, axis=1))
        total = product[at] + fold(dot_nt(terms, selector[at]))
        smooth_z[at + 1] = near_z[at + 1] - OMEGA_FINE * total / diagonal[at]
        send_halo(smooth_bufs, smooth_sems, at)

        @pl.when(at == 0)
        def _():
            send_z_low(smooth_bufs, smooth_sems)

        @pl.when(at == last)
        def _():
            send_z_high(smooth_bufs, smooth_sems)
        return carry

    lax.fori_loop(0, count, smooth, 0)

    def coarse_local(at, carry):
        value = split(smooth_z[at + 1])
        applied = split(fold(dot_nt(value, diag_high[at]) + dot_nt(value, diag_low[at])))
        own = fold(dot_nt(value, applied))
        own_block[at] = own[:, :modes] + own[:, modes:]
        picked = dot_nn(value, selector[at]).astype(jnp.bfloat16)
        for side in range(6):
            here = picked[:, side * face : (side + 1) * face]
            reach[at, side] = split(
                fold(dot_nn(here, face_high[at, side]) + dot_nn(here, face_low[at, side]))
            )
        return carry

    lax.fori_loop(0, count, coarse_local, 0)

    for side in range(6):

        @pl.when(has[side])
        def _(side=side):
            modes_copy(side, side).wait_recv()

    own_modes = modes_pack[...]
    zero_block = jnp.zeros((modes, modes), jnp.float32)

    def lane_block(value, at):
        return value[:, at * modes : (at + 1) * modes]

    along_z = (
        [lane_block(modes_halo[4], last)]
        + [lane_block(own_modes, at) for at in range(count)]
        + [lane_block(modes_halo[5], 0)]
    )
    around = []
    for at in range(count):
        sides = [lane_block(modes_halo[side], at) for side in range(4)]
        around.append(
            split(
                jnp.concatenate([along_z[at + 1]] + sides + [along_z[at], along_z[at + 2]], axis=1)
            )
        )

    smoothed_t, through = [], []
    for at in range(count):
        wait_y(smooth_bufs, smooth_sems, at)
        wait_xz(smooth_bufs, smooth_sems, at)
        blocks = [own_block[at]]
        for side in range(6):
            if side < 2:
                value = smooth_x[side, at]
            elif side < 4:
                value = smooth_y[side - 2, at]
            else:
                value = smooth_z[at + 2 * (side - 4)]
            blocks.append(product_of(dot_nt, reach[at, side], two_pieces(value)))
        coarse = jnp.concatenate(blocks, axis=1)
        coarse_out[at] = coarse
        sizes_high, sizes_low = two_pieces(jnp.abs(coarse))
        ones = jnp.ones(coarse.shape, jnp.bfloat16)
        scale = dot_nt(ones, sizes_high) + dot_nt(ones, sizes_low) + EPSILON
        coarse = two_pieces(coarse)
        applied = product_of(dot_nt, around[at], coarse)
        result = along_z[at + 1] - OMEGA_COARSE * applied / scale
        smoothed_t.append(result)
        through.append(product_of(dot_nn, split(result), coarse))

    right_rows = [1, 2, 3, 4, 0, 0]
    filler = jnp.zeros((modes, LANES - count * modes), jnp.float32)
    right[pl.ds(0, modes), pl.ds(0, LANES)] = jnp.concatenate(smoothed_t + [filler], axis=1)

    def result_copy(side, landing):
        return pltpu.make_async_remote_copy(
            src_ref=right.at[pl.ds(0, modes), pl.ds(0, LANES)],
            dst_ref=right.at[
                pl.ds(right_rows[landing] * modes, modes), pl.ds((landing + 1) * LANES, LANES)
            ],
            send_sem=result_send.at[side],
            recv_sem=result_recv.at[landing],
            device_id=target[side],
            device_id_type=MESH,
        )

    for side in range(6):

        @pl.when(has[side])
        def _(side=side):
            result_copy(side, side ^ 1).start()

    def block_of(at, which):
        return lane_block(through[at], which)

    centre = []
    for at in range(count):
        value = block_of(at, 0)
        if at < last:
            value = value + block_of(at + 1, 5)
        if at > 0:
            value = value + block_of(at - 1, 6)
        centre.append(value)
    left[:, pl.ds(0, LANES)] = jnp.concatenate(centre + [filler], axis=1)
    for side in range(4):
        pieces = [block_of(at, side + 1) for at in range(count)]
        left[:, pl.ds((side + 1) * LANES, LANES)] = jnp.concatenate(pieces + [filler], axis=1)
    low = [zero_block] * last + [block_of(0, 5)]
    left[:, pl.ds(5 * LANES, LANES)] = jnp.concatenate(low + [filler], axis=1)
    high = [block_of(last, 6)] + [zero_block] * last
    left[:, pl.ds(6 * LANES, LANES)] = jnp.concatenate(high + [filler], axis=1)

    for side in range(6):

        @pl.when(has[side])
        def _(side=side):
            result_copy(side, side).wait_recv()

    part[...] = product_of(dot_nt, split(left[...]), two_pieces(right[...]))
    gathered[gz] = part[...]
    shares = [
        pltpu.make_async_remote_copy(
            src_ref=part,
            dst_ref=gathered.at[gz],
            send_sem=sum_send.at[at],
            recv_sem=sum_recv.at[at],
            device_id={"gz": peer},
            device_id_type=MESH,
        )
        for at, peer in enumerate(peers)
    ]
    for share in shares:
        share.start()

    def finish(at, carry):
        wait_sent(near_bufs, near_sems, at)
        wait_sent(smooth_bufs, smooth_sems, at)
        return carry

    lax.fori_loop(0, count, finish, 0)
    wait_sent_z(near_bufs, near_sems)
    wait_sent_z(smooth_bufs, smooth_sems)
    for side in range(6):

        @pl.when(has[side])
        def _(side=side):
            modes_copy(side, side ^ 1).wait_send()
            result_copy(side, side ^ 1).wait_send()

    for share in shares:
        share.wait()
    total = gathered[0]
    for at in range(1, n_z):
        total = total + gathered[at]
    column_out[...] = total[:, : 5 * modes]


def per_device(sizes, near_modes, diag_blocks, face_blocks, face_rows, coarse_modes):
    count, modes, dofs = near_modes.shape[2:]
    face = face_blocks.shape[4]
    n_z = sizes[2]
    any_space = pl.BlockSpec(memory_space=pltpu.HBM)
    vmem = pl.BlockSpec(memory_space=pltpu.VMEM)
    f32, bf16 = jnp.float32, jnp.bfloat16
    dma = pltpu.SemaphoreType.DMA
    coarse_one, column = pl.pallas_call(
        functools.partial(kernel, sizes),
        out_shape=(
            jax.ShapeDtypeStruct((count, modes, 7 * modes), f32),
            jax.ShapeDtypeStruct((modes, 5 * modes), f32),
        ),
        in_specs=[any_space] * 5,
        out_specs=(vmem, vmem),
        scratch_shapes=[
            pltpu.VMEM((2, count, modes, dofs), f32),
            pltpu.VMEM((2, count, modes, dofs), f32),
            pltpu.VMEM((count + 2, modes, dofs), f32),
            pltpu.VMEM((2, count, modes, dofs), f32),
            pltpu.VMEM((2, count, modes, dofs), f32),
            pltpu.VMEM((count + 2, modes, dofs), f32),
            pltpu.VMEM((count, dofs, dofs), f32),
            pltpu.VMEM((count, 6, face, dofs), f32),
            pltpu.VMEM((6, count, face), jnp.int32),
            pltpu.VMEM((count, modes, modes), f32),
            pltpu.VMEM((count, dofs, dofs), bf16),
            pltpu.VMEM((count, dofs, dofs), bf16),
            pltpu.VMEM((count, 6, face, dofs), bf16),
            pltpu.VMEM((count, 6, face, dofs), bf16),
            pltpu.VMEM((count, dofs, 6 * face), bf16),
            pltpu.VMEM((count, modes, dofs), f32),
            pltpu.VMEM((count, 1, dofs), f32),
            pltpu.VMEM((count, 6, 2 * modes, dofs), bf16),
            pltpu.VMEM((count, modes, modes), f32),
            pltpu.VMEM((modes, LANES), f32),
            pltpu.VMEM((6, modes, LANES), f32),
            pltpu.VMEM((LANES, 7 * LANES), f32),
            pltpu.VMEM((modes, 7 * LANES), f32),
            pltpu.VMEM((modes, LANES), f32),
            pltpu.VMEM((n_z, modes, LANES), f32),
            dma((3,)),
            dma((count,)),
            dma((count,)),
            dma((6, count)),
            dma((6, count)),
            dma((6, count)),
            dma((6, count)),
            dma((6,)),
            dma((6,)),
            dma((6,)),
            dma((6,)),
            dma((n_z - 1,)),
            dma((n_z - 1,)),
        ],
        compiler_params=pltpu.CompilerParams(
            collective_id=0, has_side_effects=True, vmem_limit_bytes=2**26 - 10550 * 1024
        ),
        cost_estimate=pl.CostEstimate(flops=2 * 10**9, bytes_accessed=11 * 10**6, transcendentals=0),
    )(near_modes, diag_blocks, face_blocks, jnp.transpose(face_rows, (0, 1, 3, 2, 4)), coarse_modes)
    return coarse_one[None, None], column[None, None]


def solution(mesh):
    placed = (
        P("gx", "gy", "gz", None, None),
        P("gx", "gy", "gz", None, None),
        P("gx", "gy", "gz", None, None, None),
        P("gx", "gy", "gz", None, None),
        P("gx", "gy", "gz", None, None),
    )
    sizes = tuple(mesh.shape[axis] for axis in ("gx", "gy", "gz"))
    return jax.shard_map(
        functools.partial(per_device, sizes),
        mesh=mesh,
        in_specs=placed,
        out_specs=(P("gx", "gy", "gz", None, None), P("gx", "gy", None, None)),
        check_vma=False,
    )
```

```python
import functools

import jax
import jax.numpy as jnp
from jax import lax
from jax.experimental import pallas as pl
from jax.experimental.pallas import tpu as pltpu
from jax.sharding import PartitionSpec as P

MESH = pl.DeviceIdType.MESH
OMEGA_FINE = 2.0 / 3.0
OMEGA_COARSE = 1.0
EPSILON = 1e-06
LANES = 128
WIDTH = 4


def dot_nt(left, right, precision=None):
    return lax.dot_general(
        left, right, (((1,), (1,)), ((), ())), precision=precision, preferred_element_type=jnp.float32
    )


def dot_nn(left, right, precision=None):
    return lax.dot_general(
        left, right, (((1,), (0,)), ((), ())), precision=precision, preferred_element_type=jnp.float32
    )


def split(value):
    high = value.astype(jnp.bfloat16).astype(jnp.float32)
    return jnp.concatenate([high, value - high], axis=0).astype(jnp.bfloat16)


def two_pieces(value):
    high = value.astype(jnp.bfloat16)
    return high, (value - high.astype(jnp.float32)).astype(jnp.bfloat16)


def product_of(dot, left, right):
    return fold(dot(left, right[0]) + dot(left, right[1]))


def fold(value):
    half = value.shape[0] // 2
    return value[:half] + value[half:]


def split_into(source, high_ref, low_ref, rows, step):
    for start in range(0, rows, step):
        part = source[pl.ds(start, step)]
        high = part.astype(jnp.bfloat16)
        high_ref[pl.ds(start, step)] = high
        low_ref[pl.ds(start, step)] = (part - high.astype(jnp.float32)).astype(jnp.bfloat16)


def kernel(
    sizes,
    near_hbm,
    diag_hbm,
    face_hbm,
    rows_hbm,
    modes_hbm,
    coarse_out,
    column_out,
    near_x,
    near_y,
    near_z,
    smooth_x,
    smooth_y,
    smooth_z,
    diag_in,
    face_in,
    rows_in,
    modes_in,
    diag_high,
    diag_low,
    face_high,
    face_low,
    selector,
    product,
    diagonal,
    reach,
    own_block,
    modes_pack,
    modes_halo,
    right,
    left,
    part,
    gathered,
    load_sem,
    diag_sem,
    face_sem,
    near_send,
    near_recv,
    smooth_send,
    smooth_recv,
    modes_send,
    modes_recv,
    result_send,
    result_recv,
    sum_send,
    sum_recv,
):
    n_x, n_y, n_z = sizes
    count, modes, dofs = product.shape
    face = face_in.shape[2]
    last = count - 1
    gx, gy, gz = lax.axis_index("gx"), lax.axis_index("gy"), lax.axis_index("gz")
    has = [gx > 0, gx < n_x - 1, gy > 0, gy < n_y - 1, gz > 0, gz < n_z - 1]
    target = [
        {"gx": gx - 1},
        {"gx": gx + 1},
        {"gy": gy - 1},
        {"gy": gy + 1},
        {"gz": gz - 1},
        {"gz": gz + 1},
    ]
    width = WIDTH if n_z % WIDTH == 0 else 1
    height = n_z // width
    steps = [(step_y, step_x) for step_y in range(height) for step_x in range(width)][1:]
    steps.sort(key=lambda step: -min(step[0], height - step[0]) - min(step[1], width - step[1]))
    peers = [
        lax.rem(gz // width + step_y, height) * width + lax.rem(lax.rem(gz, width) + step_x, width)
        for step_y, step_x in steps
    ]

    loads = [
        pltpu.make_async_copy(near_hbm.at[0, 0], near_z.at[pl.ds(1, count)], load_sem.at[0]),
        pltpu.make_async_copy(rows_hbm.at[0, 0], rows_in, load_sem.at[1]),
        pltpu.make_async_copy(modes_hbm.at[0, 0], modes_in, load_sem.at[2]),
    ]
    for load in loads:
        load.start()

    def load_diag(at):
        return pltpu.make_async_copy(diag_hbm.at[0, 0, at], diag_in.at[at], diag_sem.at[at])

    def load_face(at):
        return pltpu.make_async_copy(face_hbm.at[0, 0, at], face_in.at[at], face_sem.at[at])

    for at in range(count):
        load_diag(at).start()
    for at in range(count):
        load_face(at).start()

    right[...] = jnp.zeros_like(right)

    barrier = pltpu.get_barrier_semaphore()
    for peer in peers:
        pl.semaphore_signal(barrier, inc=1, device_id={"gz": peer}, device_id_type=MESH)

    for side in range(4):

        @pl.when(has[side])
        def _(side=side):
            pl.semaphore_signal(barrier, inc=1, device_id=target[side], device_id_type=MESH)

    for side in range(2):

        @pl.when(jnp.logical_not(has[side]))
        def _(side=side):
            near_x[side] = jnp.zeros_like(near_x[side])
            smooth_x[side] = jnp.zeros_like(smooth_x[side])

        @pl.when(jnp.logical_not(has[2 + side]))
        def _(side=side):
            near_y[side] = jnp.zeros_like(near_y[side])
            smooth_y[side] = jnp.zeros_like(smooth_y[side])

        @pl.when(jnp.logical_not(has[4 + side]))
        def _(side=side):
            near_z[side * (count + 1)] = jnp.zeros((modes, dofs), jnp.float32)
            smooth_z[side * (count + 1)] = jnp.zeros((modes, dofs), jnp.float32)

    for side in range(6):

        @pl.when(jnp.logical_not(has[side]))
        def _(side=side):
            modes_halo[side] = jnp.zeros_like(modes_halo[side])

    loads[0].wait()

    met = n_z - 1
    for flag in has[:4]:
        met = met + flag.astype(jnp.int32)
    pl.semaphore_wait(barrier, met)

    def halo(bufs, sems, side, at, landing):
        buf_x, buf_y, buf_z = bufs
        send, recv = sems
        if side < 2:
            dst = buf_x.at[landing, at]
        elif side < 4:
            dst = buf_y.at[landing - 2, at]
        else:
            dst = buf_z.at[(landing - 4) * (count + 1)]
        return pltpu.make_async_remote_copy(
            src_ref=buf_z.at[at + 1],
            dst_ref=dst,
            send_sem=send.at[side, at],
            recv_sem=recv.at[landing, at],
            device_id=target[side],
            device_id_type=MESH,
        )

    def send_halo(bufs, sems, at):
        for side in (0, 1, 2, 3):

            @pl.when(has[side])
            def _(side=side):
                halo(bufs, sems, side, at, side ^ 1).start()

    def send_z_low(bufs, sems):
        @pl.when(has[4])
        def _():
            halo(bufs, sems, 4, 0, 5).start()

    def send_z_high(bufs, sems):
        @pl.when(has[5])
        def _():
            halo(bufs, sems, 5, last, 4).start()

    def wait_y(bufs, sems, at):
        for side in (2, 3):

            @pl.when(has[side])
            def _(side=side):
                halo(bufs, sems, side, at, side).wait_recv()

    def wait_xz(bufs, sems, at):
        for side in (0, 1):

            @pl.when(has[side])
            def _(side=side):
                halo(bufs, sems, side, at, side).wait_recv()

        @pl.when(has[4] & (at == 0))
        def _():
            halo(bufs, sems, 4, last, 4).wait_recv()

        @pl.when(has[5] & (at == last))
        def _():
            halo(bufs, sems, 5, 0, 5).wait_recv()

    def wait_sent(bufs, sems, at):
        for side in (0, 1, 2, 3):

            @pl.when(has[side])
            def _(side=side):
                halo(bufs, sems, side, at, side ^ 1).wait_send()


    def wait_sent_z(bufs, sems):
        @pl.when(has[4])
        def _():
            halo(bufs, sems, 4, 0, 5).wait_send()

        @pl.when(has[5])
        def _():
            halo(bufs, sems, 5, last, 4).wait_send()

    near_bufs, near_sems = (near_x, near_y, near_z), (near_send, near_recv)
    smooth_bufs, smooth_sems = (smooth_x, smooth_y, smooth_z), (smooth_send, smooth_recv)

    def send_near(at, carry):
        send_halo(near_bufs, near_sems, at)
        return carry

    lax.fori_loop(0, count, send_near, 0)
    send_z_low(near_bufs, near_sems)
    send_z_high(near_bufs, near_sems)

    loads[2].wait()
    pieces = [modes_in[at].T for at in range(count)]
    pieces.append(jnp.zeros((modes, LANES - count * modes), jnp.float32))
    modes_pack[...] = jnp.concatenate(pieces, axis=1)
    def modes_copy(side, landing):
        return pltpu.make_async_remote_copy(
            src_ref=modes_pack,
            dst_ref=modes_halo.at[landing],
            send_sem=modes_send.at[side],
            recv_sem=modes_recv.at[landing],
            device_id=target[side],
            device_id_type=MESH,
        )

    for side in range(6):

        @pl.when(has[side])
        def _(side=side):
            modes_copy(side, side ^ 1).start()

    loads[1].wait()

    def build_selector(at, carry):
        for side in range(6):
            chosen = rows_in[side, pl.ds(at, 1), :]
            for start in range(0, dofs, LANES):
                row = lax.broadcasted_iota(jnp.int32, (LANES, face), 0) + start
                hit = jnp.where(row == chosen, 1.0, 0.0).astype(jnp.bfloat16)
                selector[at, pl.ds(start, LANES), pl.ds(side * face, face)] = hit
        return carry

    lax.fori_loop(0, count, build_selector, 0)
    def own_product(at, carry):
        load_diag(at).wait()
        split_into(diag_in.at[at], diag_high.at[at], diag_low.at[at], dofs, 64)
        here = []
        for start in range(0, dofs, LANES):
            block = diag_in[at, pl.ds(start, LANES), pl.ds(start, LANES)]
            row = lax.broadcasted_iota(jnp.int32, (LANES, LANES), 0)
            col = lax.broadcasted_iota(jnp.int32, (LANES, LANES), 1)
            here.append(jnp.sum(jnp.where(row == col, block, 0.0), axis=0, keepdims=True))
        diagonal[at] = jnp.concatenate(here, axis=1)
        value = split(near_z[at + 1])
        product[at] = fold(dot_nt(value, diag_high[at]) + dot_nt(value, diag_low[at]))
        return carry

    lax.fori_loop(0, count, own_product, 0)

    def split_faces(at, carry):
        load_face(at).wait()
        for side in range(6):
            split_into(
                face_in.at[at, side], face_high.at[at, side], face_low.at[at, side], face, 64
            )
        return carry

    lax.fori_loop(0, count, split_faces, 0)

    def smooth(at, carry):
        wait_y(near_bufs, near_sems, at)
        wait_xz(near_bufs, near_sems, at)

        terms = []
        for side in range(6):
            if side < 2:
                value = near_x[side, at]
            elif side < 4:
                value = near_y[side - 2, at]
            else:
                value = near_z[at + 2 * (side - 4)]
            value = split(value)
            terms.append(
                fold(dot_nt(value, face_high[at, side]) + dot_nt(value, face_low[at, side]))
            )
        terms = split(jnp.concatenate(terms, axis=1))
        total = product[at] + fold(dot_nt(terms, selector[at]))
        smooth_z[at + 1] = near_z[at + 1] - OMEGA_FINE * total / diagonal[at]
        send_halo(smooth_bufs, smooth_sems, at)

        @pl.when(at == 0)
        def _():
            send_z_low(smooth_bufs, smooth_sems)

        @pl.when(at == last)
        def _():
            send_z_high(smooth_bufs, smooth_sems)
        return carry

    lax.fori_loop(0, count, smooth, 0)

    def coarse_local(at, carry):
        value = split(smooth_z[at + 1])
        applied = split(fold(dot_nt(value, diag_high[at]) + dot_nt(value, diag_low[at])))
        own = fold(dot_nt(value, applied))
        own_block[at] = own[:, :modes] + own[:, modes:]
        picked = dot_nn(value, selector[at]).astype(jnp.bfloat16)
        for side in range(6):
            here = picked[:, side * face : (side + 1) * face]
            reach[at, side] = split(
                fold(dot_nn(here, face_high[at, side]) + dot_nn(here, face_low[at, side]))
            )
        return carry

    lax.fori_loop(0, count, coarse_local, 0)

    for side in range(6):

        @pl.when(has[side])
        def _(side=side):
            modes_copy(side, side).wait_recv()

    own_modes = modes_pack[...]
    zero_block = jnp.zeros((modes, modes), jnp.float32)

    def lane_block(value, at):
        return value[:, at * modes : (at + 1) * modes]

    along_z = (
        [lane_block(modes_halo[4], last)]
        + [lane_block(own_modes, at) for at in range(count)]
        + [lane_block(modes_halo[5], 0)]
    )
    around = []
    for at in range(count):
        sides = [lane_block(modes_halo[side], at) for side in range(4)]
        around.append(
            split(
                jnp.concatenate([along_z[at + 1]] + sides + [along_z[at], along_z[at + 2]], axis=1)
            )
        )

    smoothed_t, through = [], []
    for at in range(count):
        wait_y(smooth_bufs, smooth_sems, at)
        wait_xz(smooth_bufs, smooth_sems, at)
        blocks = [own_block[at]]
        for side in range(6):
            if side < 2:
                value = smooth_x[side, at]
            elif side < 4:
                value = smooth_y[side - 2, at]
            else:
                value = smooth_z[at + 2 * (side - 4)]
            blocks.append(product_of(dot_nt, reach[at, side], two_pieces(value)))
        coarse = jnp.concatenate(blocks, axis=1)
        coarse_out[at] = coarse
        sizes_high, sizes_low = two_pieces(jnp.abs(coarse))
        ones = jnp.ones(coarse.shape, jnp.bfloat16)
        scale = dot_nt(ones, sizes_high) + dot_nt(ones, sizes_low) + EPSILON
        coarse = two_pieces(coarse)
        applied = product_of(dot_nt, around[at], coarse)
        result = along_z[at + 1] - OMEGA_COARSE * applied / scale
        smoothed_t.append(result)
        through.append(product_of(dot_nn, split(result), coarse))

    right_rows = [1, 2, 3, 4, 0, 0]
    filler = jnp.zeros((modes, LANES - count * modes), jnp.float32)
    right[pl.ds(0, modes), pl.ds(0, LANES)] = jnp.concatenate(smoothed_t + [filler], axis=1)

    def result_copy(side, landing):
        return pltpu.make_async_remote_copy(
            src_ref=right.at[pl.ds(0, modes), pl.ds(0, LANES)],
            dst_ref=right.at[
                pl.ds(right_rows[landing] * modes, modes), pl.ds((landing + 1) * LANES, LANES)
            ],
            send_sem=result_send.at[side],
            recv_sem=result_recv.at[landing],
            device_id=target[side],
            device_id_type=MESH,
        )

    for side in range(6):

        @pl.when(has[side])
        def _(side=side):
            result_copy(side, side ^ 1).start()

    def block_of(at, which):
        return lane_block(through[at], which)

    centre = []
    for at in range(count):
        value = block_of(at, 0)
        if at < last:
            value = value + block_of(at + 1, 5)
        if at > 0:
            value = value + block_of(at - 1, 6)
        centre.append(value)
    left[:, pl.ds(0, LANES)] = jnp.concatenate(centre + [filler], axis=1)
    for side in range(4):
        pieces = [block_of(at, side + 1) for at in range(count)]
        left[:, pl.ds((side + 1) * LANES, LANES)] = jnp.concatenate(pieces + [filler], axis=1)
    low = [zero_block] * last + [block_of(0, 5)]
    left[:, pl.ds(5 * LANES, LANES)] = jnp.concatenate(low + [filler], axis=1)
    high = [block_of(last, 6)] + [zero_block] * last
    left[:, pl.ds(6 * LANES, LANES)] = jnp.concatenate(high + [filler], axis=1)

    for side in range(6):

        @pl.when(has[side])
        def _(side=side):
            result_copy(side, side).wait_recv()

    part[...] = product_of(dot_nt, split(left[...]), two_pieces(right[...]))
    gathered[gz] = part[...]
    shares = [
        pltpu.make_async_remote_copy(
            src_ref=part,
            dst_ref=gathered.at[gz],
            send_sem=sum_send.at[at],
            recv_sem=sum_recv.at[at],
            device_id={"gz": peer},
            device_id_type=MESH,
        )
        for at, peer in enumerate(peers)
    ]
    for share in shares:
        share.start()

    def finish(at, carry):
        wait_sent(near_bufs, near_sems, at)
        wait_sent(smooth_bufs, smooth_sems, at)
        return carry

    lax.fori_loop(0, count, finish, 0)
    wait_sent_z(near_bufs, near_sems)
    wait_sent_z(smooth_bufs, smooth_sems)
    for side in range(6):

        @pl.when(has[side])
        def _(side=side):
            modes_copy(side, side ^ 1).wait_send()
            result_copy(side, side ^ 1).wait_send()

    for share in shares:
        share.wait()
    total = gathered[0]
    for at in range(1, n_z):
        total = total + gathered[at]
    column_out[...] = total[:, : 5 * modes]


def per_device(sizes, near_modes, diag_blocks, face_blocks, face_rows, coarse_modes):
    count, modes, dofs = near_modes.shape[2:]
    face = face_blocks.shape[4]
    n_z = sizes[2]
    any_space = pl.BlockSpec(memory_space=pltpu.HBM)
    vmem = pl.BlockSpec(memory_space=pltpu.VMEM)
    f32, bf16 = jnp.float32, jnp.bfloat16
    dma = pltpu.SemaphoreType.DMA
    coarse_one, column = pl.pallas_call(
        functools.partial(kernel, sizes),
        out_shape=(
            jax.ShapeDtypeStruct((count, modes, 7 * modes), f32),
            jax.ShapeDtypeStruct((modes, 5 * modes), f32),
        ),
        in_specs=[any_space] * 5,
        out_specs=(vmem, vmem),
        scratch_shapes=[
            pltpu.VMEM((2, count, modes, dofs), f32),
            pltpu.VMEM((2, count, modes, dofs), f32),
            pltpu.VMEM((count + 2, modes, dofs), f32),
            pltpu.VMEM((2, count, modes, dofs), f32),
            pltpu.VMEM((2, count, modes, dofs), f32),
            pltpu.VMEM((count + 2, modes, dofs), f32),
            pltpu.VMEM((count, dofs, dofs), f32),
            pltpu.VMEM((count, 6, face, dofs), f32),
            pltpu.VMEM((6, count, face), jnp.int32),
            pltpu.VMEM((count, modes, modes), f32),
            pltpu.VMEM((count, dofs, dofs), bf16),
            pltpu.VMEM((count, dofs, dofs), bf16),
            pltpu.VMEM((count, 6, face, dofs), bf16),
            pltpu.VMEM((count, 6, face, dofs), bf16),
            pltpu.VMEM((count, dofs, 6 * face), bf16),
            pltpu.VMEM((count, modes, dofs), f32),
            pltpu.VMEM((count, 1, dofs), f32),
            pltpu.VMEM((count, 6, 2 * modes, dofs), bf16),
            pltpu.VMEM((count, modes, modes), f32),
            pltpu.VMEM((modes, LANES), f32),
            pltpu.VMEM((6, modes, LANES), f32),
            pltpu.VMEM((LANES, 7 * LANES), f32),
            pltpu.VMEM((modes, 7 * LANES), f32),
            pltpu.VMEM((modes, LANES), f32),
            pltpu.VMEM((n_z, modes, LANES), f32),
            dma((3,)),
            dma((count,)),
            dma((count,)),
            dma((6, count)),
            dma((6, count)),
            dma((6, count)),
            dma((6, count)),
            dma((6,)),
            dma((6,)),
            dma((6,)),
            dma((6,)),
            dma((n_z - 1,)),
            dma((n_z - 1,)),
        ],
        compiler_params=pltpu.CompilerParams(
            collective_id=0, has_side_effects=True, vmem_limit_bytes=2**26 - 10550 * 1024
        ),
        cost_estimate=pl.CostEstimate(flops=2 * 10**9, bytes_accessed=11 * 10**6, transcendentals=0),
    )(near_modes, diag_blocks, face_blocks, jnp.transpose(face_rows, (0, 1, 3, 2, 4)), coarse_modes)
    return coarse_one[None, None], column[None, None]


def solution(mesh):
    placed = (
        P("gx", "gy", "gz", None, None),
        P("gx", "gy", "gz", None, None),
        P("gx", "gy", "gz", None, None, None),
        P("gx", "gy", "gz", None, None),
        P("gx", "gy", "gz", None, None),
    )
    sizes = tuple(mesh.shape[axis] for axis in ("gx", "gy", "gz"))
    return jax.shard_map(
        functools.partial(per_device, sizes),
        mesh=mesh,
        in_specs=placed,
        out_specs=(P("gx", "gy", "gz", None, None), P("gx", "gy", None, None)),
        check_vma=False,
    )
```
